256 devices in a mesh: row: 16 (over y_hi, z), col: 16 (over y_lo, x, core).
Axes of the slice: x: 4, y: 4 (y_hi: 2, y_lo: 2; y = y_hi * 2 + y_lo), z: 8, core: 2. Of those that a mesh axis runs over, the one named last changes fastest.
Arguments:
- features: bfloat16 [65536, 256], P(('col', 'row')), may hold values from -6 to 6
- adj_tiles: bfloat16 [16, 512, 12, 128, 128], P('col', 'row'), may hold values from -0.0625 to 0.0625
- tile_cols: int32 [16, 512, 12], P('col', 'row'), may hold values from 0 to 31
- tile_count: int32 [16, 512], P('col', 'row'), may hold values from 1 to 12, as said below
- weight: bfloat16 [256, 256], replicated, may hold values from -0.375 to 0.375
- cotangent: bfloat16 [65536, 256], P(('row', 'col')), may hold values from -6 to 6
Outputs:
- activation: bfloat16 [65536, 256], P(('row', 'col'))
- feature_grad: bfloat16 [65536, 256], P(('col', 'row'))
The draws below stay inside these ranges and needn't reach their ends.
Inputs may be any that keep to these rules, and one draw needn't show every extreme that they name: `tile_count`: some tile row of some block column has all 12 slots live; the number of live slots differs strongly between blocks.
All inputs are finite; a program needn't handle non-finite values.
Results may differ from the reference program's by a relative error of at most 0.0065.
Values may be sent and summed in bfloat16 or wider, within the bound.
No kernel may reach another device: no remote copies, remote signals or barrier semaphores. Data moves between devices by JAX's collectives and lax.ppermute only.
A program may use at most 128 MiB of HBM per device.

```python
import jax
import jax.numpy as jnp
from jax import lax

F = 256
TILE = 128
SLOTS = 12
NT = 512
TROWS = 32
TCOLS = 32
N = 65536
N_ROW = 16
N_COL = 16


def draw_tile_count(key, part):
    key = jax.random.fold_in(key, 11)
    key_base, key_level, key_spot = jax.random.split(key, 3)
    base = jax.random.randint(key_base, (N_COL, N_ROW, TROWS), 1, SLOTS + 1)
    level = jax.random.randint(key_level, (N_COL, N_ROW, 1), 1, 5)
    counts = jnp.maximum(base * level // 4, 1).reshape(-1)
    spot = jax.random.randint(key_spot, (), 0, N_COL * N_ROW * TROWS)
    counts = counts.at[spot].set(SLOTS)
    return counts.reshape(N_COL, NT).astype(jnp.int32)


def touch_ends(result, own_key, least, largest):
    longest = result.shape.index(max(result.shape))
    spots = []
    for shift in (0, 1):
        where = [jax.random.randint(jax.random.fold_in(own_key, axis), (), 0, length) for axis, length in enumerate(result.shape)]
        where[longest] = (where[longest] + shift) % result.shape[longest]
        spots.append(tuple(where))
    return result.at[spots[0]].set(least).at[spots[1]].set(largest)


def levels(stream_key, extent, cuts, least, high):
    loudness = 1.0
    for dim, blocks in cuts:
        draws = jax.random.uniform(jax.random.fold_in(jax.random.fold_in(stream_key, 6), dim), (blocks,), jnp.float32, least / len(cuts), high / len(cuts))
        loudness = loudness * jnp.repeat(jnp.exp(draws), extent[dim] // blocks).reshape((-1,) + (1,) * (len(extent) - 1 - dim))
    return loudness


def centred(rng, dims, spread, limit, cuts=(), kind=jnp.bfloat16):
    gain = levels(rng, dims, cuts, -0.22, 0.18) if cuts else 1.0
    array = jax.random.normal(rng, dims, jnp.float32) * spread * gain
    return jnp.minimum(jnp.maximum(array, -limit), limit).astype(kind)


def setup_inputs(seed: int = 0) -> dict:
    arg_keys = jax.random.split(jax.random.key(seed), 7)
    return {
        "features": centred(arg_keys[0], (N, F), 1.0, 6.0, ((0, 256),)),
        "adj_tiles": centred(arg_keys[1], (N_COL, NT, SLOTS, TILE, TILE), (SLOTS * TILE * N_COL // 3) ** -0.5, 0.0625, ((0, 16), (1, 16))),
        "tile_cols": touch_ends(jax.random.randint(arg_keys[2], (N_COL, NT, SLOTS), 0, TCOLS), jax.random.fold_in(arg_keys[2], 1), 0, TCOLS - 1).astype(jnp.int32),
        "tile_count": draw_tile_count(jax.random.fold_in(arg_keys[6], 71), 0),
        "weight": centred(arg_keys[4], (F, F), F ** -0.5, 0.375),
        "cotangent": centred(arg_keys[5], (N, F), 1.0, 6.0, ((0, 256),)),
    }


def silu_slope(values):
    sigma = jax.nn.sigmoid(values)
    return sigma * (1.0 + values * (1.0 - sigma))


def gather_product(adj_tiles, tile_cols, counts, source):
    rows, slots, tile_size, _ = adj_tiles.shape
    width = source.shape[-1]
    blocks = source.reshape(-1, tile_size, width)
    live_slots = jnp.arange(slots, dtype=jnp.int32)[None, :] < counts[:, None]
    picked = jnp.where(live_slots[:, :, None, None], blocks[tile_cols], jnp.zeros((), source.dtype))
    product = jnp.einsum('tkab,tkbf->taf', adj_tiles.astype(jnp.float32), picked.astype(jnp.float32))
    return product.reshape(rows * tile_size, width)


def spread_back(adj_tiles, tile_cols, counts, grads, col_tiles):
    rows, slots, tile_size, _ = adj_tiles.shape
    width = grads.shape[-1]
    step_rows = 8
    block_count = rows // step_rows
    live_slots = jnp.arange(slots, dtype=jnp.int32)[None, :] < counts[:, None]
    targets = jnp.where(live_slots, tile_cols, col_tiles).astype(jnp.int32)

    def one_block(total, inputs):
        block_tiles, block_targets, block_grads = inputs
        contrib = jnp.einsum('tkab,taf->tkbf', block_tiles.astype(jnp.float32),
                             block_grads.reshape(step_rows, tile_size, width).astype(jnp.float32))
        summed = jax.ops.segment_sum(contrib.reshape(step_rows * slots, tile_size, width),
                                     block_targets.reshape(-1), num_segments=col_tiles + 1)
        return total + summed[:col_tiles], None

    start_total = jnp.zeros((col_tiles, tile_size, width), jnp.float32)
    total, _ = lax.scan(one_block, start_total,
                        (adj_tiles.reshape(block_count, step_rows, slots, tile_size, tile_size),
                         targets.reshape(block_count, step_rows, slots),
                         grads.reshape(block_count, step_rows * tile_size, width)))
    return total.reshape(col_tiles * tile_size, width)


def reference(features, adj_tiles, tile_cols, tile_count, weight, cotangent):
    panel = TCOLS * TILE

    def forward_col(total, inputs):
        col_tiles, col_index, col_counts, which = inputs
        source = lax.dynamic_slice_in_dim(features, (which * panel).astype(jnp.int32), panel, 0)

        def by_block(blocked):
            return gather_product(blocked[0], blocked[1], blocked[2], source)

        parts = lax.map(by_block, (col_tiles.reshape(N_ROW, TROWS, SLOTS, TILE, TILE),
                                   col_index.reshape(N_ROW, TROWS, SLOTS),
                                   col_counts.reshape(N_ROW, TROWS)))
        return total + parts.reshape(N, F), None

    summed, _ = lax.scan(forward_col, jnp.zeros((N, F), jnp.float32),
                         (adj_tiles, tile_cols, tile_count, jnp.arange(N_COL, dtype=jnp.int32)))
    aggregated = summed.astype(jnp.bfloat16)
    pre = jnp.dot(aggregated, weight, preferred_element_type=jnp.float32)
    activation = jax.nn.silu(pre).astype(jnp.bfloat16)
    pre_grad = (cotangent.astype(jnp.float32) * silu_slope(pre)).astype(jnp.bfloat16)
    agg_grad = jnp.dot(pre_grad, weight.T, preferred_element_type=jnp.float32).astype(jnp.bfloat16)

    def backward_col(inputs):
        col_tiles, col_index, col_counts = inputs
        return spread_back(col_tiles, col_index, col_counts, agg_grad, TCOLS)

    grads = lax.map(backward_col, (adj_tiles, tile_cols, tile_count))
    feature_grad = grads.reshape(N, F).astype(jnp.bfloat16)
    return activation, feature_grad
```

```python
import functools

import jax
import jax.numpy as jnp
from jax import lax
from jax.experimental import pallas as pl
from jax.experimental.pallas import tpu as pltpu
from jax.sharding import Mesh
from jax.sharding import PartitionSpec as P

BF = jnp.bfloat16
F32 = jnp.float32
SM = pl.BlockSpec(memory_space=pltpu.SMEM)
VM = pl.BlockSpec(memory_space=pltpu.VMEM)
ANY = pl.BlockSpec(memory_space=pl.ANY)
NZ, NY, NX = 8, 2, 4
TILE, F, SLOTS, TROWS, TCOLS = 128, 256, 12, 32, 32
HALF = TROWS // 2
DEPTH = 4
VMEM_LIMIT = 40 << 20


def shift(value, axis, size, step):
    return lax.ppermute(value, axis, [(i, (i + step) % size) for i in range(size)])


def swap(value, axis):
    return lax.ppermute(value, axis, [(0, 1), (1, 0)])


def plane_send(value, dy, dx):
    pairs = []
    for y in range(NY):
        for x in range(NX):
            pairs.append((y * NX + x, (y + dy) % NY * NX + (x + dx) % NX))
    return lax.ppermute(value, ("yl", "x"), pairs)


PLANE = [(dy, dx) for dy in range(NY) for dx in range(NX)]


def tile_row(u, core):
    return 4 * (u >> 1) + 2 * core + (u & 1)


def fetch_pieces(at_ref, pieces, held, sem):
    copies = []
    for k, piece in enumerate(pieces):
        copies.append(
            pltpu.make_async_copy(piece, held.at[pl.ds(at_ref[k], piece.shape[0])], sem.at[k])
        )
    for copy in copies:
        copy.start()
    return copies


def stream_rows(core, adj_ref, slab, sem, work):
    def row_copy(u):
        slot = lax.rem(u, DEPTH)
        return pltpu.make_async_copy(adj_ref.at[tile_row(u, core)], slab.at[slot], sem.at[slot])

    for u in range(DEPTH - 1):
        row_copy(jnp.int32(u)).start()

    def step(u, carry):
        @pl.when(u + DEPTH - 1 < HALF)
        def _():
            row_copy(u + DEPTH - 1).start()

        row_copy(u).wait()
        work(u, slab.at[lax.rem(u, DEPTH)])
        return carry

    return step


def forward_body(core_ref, at_ref, cols_ref, counts_ref, adj_ref, *rest, n):
    pieces = rest[:n]
    out_ref, panel, slab, piece_sem, row_sem = rest[n:]
    core = core_ref[0]
    copies = fetch_pieces(at_ref, pieces, panel, piece_sem)

    def work(u, tiles):
        t = tile_row(u, core)
        count = counts_ref[t]
        pairs = (count + 1) >> 1
        for p in range(1, SLOTS // 2 + 1):

            @pl.when(pairs == p)
            def _(p=p):
                left = [tiles[s] for s in range(2 * p)]
                left[-1] = jnp.where(count == 2 * p, left[-1], jnp.zeros_like(left[-1]))
                right = [panel[cols_ref[t * SLOTS + s]] for s in range(2 * p)]
                out_ref[u] = jnp.dot(
                    jnp.concatenate(left, 1),
                    jnp.concatenate(right, 0),
                    preferred_element_type=F32,
                ).astype(out_ref.dtype)

    step = stream_rows(core, adj_ref, slab, row_sem, work)
    for copy in copies:
        copy.wait()
    lax.fori_loop(0, HALF, step, 0)


def forward(core, at, cols, counts, adj, pieces):
    n = len(pieces)
    return pl.pallas_call(
        functools.partial(forward_body, n=n),
        out_shape=jax.ShapeDtypeStruct((HALF, TILE, F), BF),
        in_specs=[SM, SM, SM, SM, ANY] + [ANY] * n,
        out_specs=VM,
        scratch_shapes=[
            pltpu.VMEM((TCOLS, TILE, F), BF),
            pltpu.VMEM((DEPTH, SLOTS, TILE, TILE), BF),
            pltpu.SemaphoreType.DMA((n,)),
            pltpu.SemaphoreType.DMA((DEPTH,)),
        ],
        compiler_params=pltpu.CompilerParams(vmem_limit_bytes=VMEM_LIMIT),
        cost_estimate=pl.CostEstimate(flops=4 * 10**9, bytes_accessed=9 << 20, transcendentals=0),
        name="forward",
    )(core, at, cols, counts, adj, *pieces)


def backward_body(core_ref, at_ref, send_ref, cols_ref, counts_ref, adj_ref, *rest, n, first):
    pieces = rest[:n]
    if first:
        out_ref, held, slab, piece_sem, row_sem = rest[n:]
        acc = out_ref
    else:
        prior_ref = rest[n]
        m = len(SENDS)
        outs = rest[n + 1 : n + 1 + m]
        held, slab, piece_sem, row_sem, acc = rest[n + 1 + m :]
    core = core_ref[0]
    copies = fetch_pieces(at_ref, pieces, held, piece_sem)

    def work(u, tiles):
        t = tile_row(u, core)
        count = counts_ref[t]
        pairs = (count + 1) >> 1
        for p in range(1, SLOTS // 2 + 1):

            @pl.when(pairs == p)
            def _(p=p):
                grad = held[u]
                for q in range(p):
                    a0, a1 = tiles[2 * q], tiles[2 * q + 1]
                    if q == p - 1:
                        a1 = jnp.where(count == 2 * p, a1, jnp.zeros_like(a1))
                    terms = jnp.dot(grad, jnp.concatenate([a0, a1], 1), preferred_element_type=F32)
                    acc[cols_ref[t * SLOTS + 2 * q]] += terms[:, :TILE]
                    acc[cols_ref[t * SLOTS + 2 * q + 1]] += terms[:, TILE:]

    step = stream_rows(core, adj_ref, slab, row_sem, work)
    if first:
        acc[...] = jnp.zeros_like(acc)
    else:
        acc[...] = prior_ref[...]
    for copy in copies:
        copy.wait()
    lax.fori_loop(0, HALF, step, 0)
    if not first:
        for k, (out, (_, tiles)) in enumerate(zip(outs, SENDS)):
            for y in range(2):
                for i, tile in enumerate(tiles):
                    out[y, i] = acc[send_ref[k * 2 + y] + tile].astype(BF)


SENDS = [(4, (0,)), (4, (1,)), (3, (0, 1)), (-3, (0, 1)), (2, (0, 1)), (-2, (0, 1)), (1, (0, 1)), (-1, (0, 1)), (0, (0, 1))]


def backward(core, at, send, cols, counts, adj, pieces, prior=None):
    n = len(pieces)
    first = prior is None
    scratch = [
        pltpu.VMEM((HALF, F, TILE), BF),
        pltpu.VMEM((DEPTH, SLOTS, TILE, TILE), BF),
        pltpu.SemaphoreType.DMA((n,)),
        pltpu.SemaphoreType.DMA((DEPTH,)),
    ]
    if first:
        out_shape = jax.ShapeDtypeStruct((TCOLS, F, TILE), F32)
        out_specs = VM
        extra = []
    else:
        out_shape = [jax.ShapeDtypeStruct((2, len(tiles), F, TILE), BF) for _, tiles in SENDS]
        out_specs = [VM] * len(SENDS)
        scratch.append(pltpu.VMEM((TCOLS, F, TILE), F32))
        extra = [prior]
    return pl.pallas_call(
        functools.partial(backward_body, n=n, first=first),
        out_shape=out_shape,
        in_specs=[SM, SM, SM, SM, SM, ANY] + [ANY] * n + [VM] * len(extra),
        out_specs=out_specs,
        scratch_shapes=scratch,
        compiler_params=pltpu.CompilerParams(vmem_limit_bytes=VMEM_LIMIT),
        cost_estimate=pl.CostEstimate(flops=4 * 10**9, bytes_accessed=9 << 20, transcendentals=0),
        name="backward",
    )(core, at, send, cols, counts, adj, *pieces, *extra)


def pair_add_body(at_ref, mine_ref, other_ref, *outs):
    for k, out in enumerate(outs):
        rows = pl.ds(at_ref[k], 2)
        out[...] = (mine_ref[rows].astype(F32) + other_ref[rows].astype(F32)).astype(BF)


def pair_add(at, mine, other):
    return pl.pallas_call(
        pair_add_body,
        out_shape=[jax.ShapeDtypeStruct((2, TILE, F), BF)] * len(PLANE),
        in_specs=[SM, VM, VM],
        out_specs=[VM] * len(PLANE),
        compiler_params=pltpu.CompilerParams(vmem_limit_bytes=VMEM_LIMIT),
        name="pair_add",
    )(at, mine, other)


def middle_body(*refs):
    n = len(PLANE)
    pieces = refs[:n]
    weight_ref, cotangent_ref, act_ref, grad_ref = refs[n:]
    total = pieces[0][...].astype(F32)
    for piece in pieces[1:]:
        total = total + piece[...].astype(F32)
    aggregated = total.astype(BF).reshape(2 * TILE, F)
    weight = weight_ref[...]
    pre = jnp.dot(aggregated, weight, preferred_element_type=F32)
    sigma = jax.nn.sigmoid(pre)
    act_ref[...] = (pre * sigma).astype(BF)
    slope = sigma * (1.0 + pre * (1.0 - sigma))
    pre_grad = (cotangent_ref[...].astype(F32) * slope).astype(BF)
    grad = lax.dot_general(
        weight, pre_grad, (((1,), (1,)), ((), ())), preferred_element_type=F32
    ).astype(BF)
    grad_ref[0] = grad[:, :TILE]
    grad_ref[1] = grad[:, TILE:]


def middle(pieces, weight, cotangent):
    return pl.pallas_call(
        middle_body,
        out_shape=[
            jax.ShapeDtypeStruct((2 * TILE, F), BF),
            jax.ShapeDtypeStruct((2, F, TILE), BF),
        ],
        in_specs=[VM] * (len(pieces) + 2),
        out_specs=[VM, VM],
        compiler_params=pltpu.CompilerParams(vmem_limit_bytes=VMEM_LIMIT),
        name="middle",
    )(*pieces, weight, cotangent)


def finish_body(a_ref, b_ref, out_ref):
    total = a_ref[...].astype(F32) + b_ref[...].astype(F32)
    for i in range(2):
        out_ref[pl.ds(i * TILE, TILE), :] = total[i].T.astype(BF)


def finish(a, b):
    return pl.pallas_call(
        finish_body,
        out_shape=jax.ShapeDtypeStruct((2 * TILE, F), BF),
        in_specs=[VM, VM],
        out_specs=VM,
        name="finish",
    )(a, b)


def add(*terms):
    total = terms[0].astype(F32)
    for term in terms[1:]:
        total = total + term.astype(F32)
    return total.astype(BF)


def local(features, adj_tiles, tile_cols, tile_count, weight, cotangent):
    adj = adj_tiles[0]
    cols = tile_cols[0].reshape(-1)
    counts = tile_count[0].reshape(-1)
    yh, z = lax.axis_index("yh"), lax.axis_index("z")
    yl, x, core = lax.axis_index("yl"), lax.axis_index("x"), lax.axis_index("c")
    mine = jnp.reshape(core, (1,)).astype(jnp.int32)
    other = 1 - mine

    own = features.reshape(2, TILE, F)
    pieces, places = [], []

    def keep(piece, half, step, tile=0):
        pieces.append(piece)
        places.append(2 * (half * NZ + (z - step) % NZ) + tile)

    far = swap(own, "yh")
    for block, half in ((own, yh), (far, 1 - yh)):
        keep(block, half, 0)
        up = down = block
        for step in range(1, NZ // 2):
            up, down = shift(up, "z", NZ, 1), shift(down, "z", NZ, -1)
            keep(up, half, step)
            keep(down, half, -step)
        keep(shift(up[:1], "z", NZ, 1), half, NZ // 2, 0)
        keep(shift(down[1:], "z", NZ, -1), half, NZ // 2, 1)
    at = jnp.stack(places).astype(jnp.int32)

    for_other = forward(other, at, cols, counts, adj, pieces)
    theirs = swap(for_other, "c")
    for_mine = forward(mine, at, cols, counts, adj, pieces)
    dests = jnp.stack([2 * ((yl + dy) % NY * NX + (x + dx) % NX) for dy, dx in PLANE]).astype(jnp.int32)
    parts = pair_add(dests, for_mine, theirs)
    parts = [parts[0]] + [plane_send(part, dy, dx) for part, (dy, dx) in list(zip(parts, PLANE))[1:]]
    activation, grad = middle(parts, weight, cotangent)

    grads = [grad] + [plane_send(grad, dy, dx) for dy, dx in PLANE[1:]]
    grad_at = jnp.stack([2 * ((yl - dy) % NY * NX + (x - dx) % NX) for dy, dx in PLANE]).astype(jnp.int32)
    grads_other = [swap(piece, "c") for piece in grads]
    send = jnp.stack(
        [2 * (half * NZ + (z + step) % NZ) for step, _ in SENDS for half in (yh, 1 - yh)]
    ).astype(jnp.int32)
    half_sum = backward(mine, grad_at, send, cols, counts, adj, grads)
    up4, down4, up3, down3, up2, down2, up1, down1, kept = backward(
        other, grad_at, send, cols, counts, adj, grads_other, half_sum
    )

    nil = jnp.zeros_like(up4)
    up = shift(up4, "z", NZ, 1)
    down = shift(down4, "z", NZ, -1)
    up = shift(add(up3, jnp.concatenate([up, nil], 1)), "z", NZ, 1)
    down = shift(add(down3, jnp.concatenate([nil, down], 1)), "z", NZ, -1)
    up = shift(add(up2, up), "z", NZ, 1)
    down = shift(add(down2, down), "z", NZ, -1)
    up = shift(add(up1, up), "z", NZ, 1)
    down = shift(add(down1, down), "z", NZ, -1)
    away = swap(add(kept[1], up[1], down[1]), "yh")
    feature_grad = finish(add(kept[0], up[0], down[0]), away)
    return activation, feature_grad


def solution(mesh):
    fine = Mesh(mesh.devices.reshape(2, NZ, NY, NX, 2), ("yh", "z", "yl", "x", "c"))
    row, col = ("yh", "z"), ("yl", "x", "c")
    in_specs = (
        P(col + row, None),
        P(col, row, None, None, None),
        P(col, row, None),
        P(col, row),
        P(),
        P(row + col, None),
    )
    out_specs = (P(row + col, None), P(col + row, None))
    return jax.shard_map(local, mesh=fine, in_specs=in_specs, out_specs=out_specs, check_vma=False)
```

```python
import functools

import jax
import jax.numpy as jnp
from jax import lax
from jax.experimental import pallas as pl
from jax.experimental.pallas import tpu as pltpu
from jax.sharding import Mesh
from jax.sharding import PartitionSpec as P

BF = jnp.bfloat16
F32 = jnp.float32
SM = pl.BlockSpec(memory_space=pltpu.SMEM)
VM = pl.BlockSpec(memory_space=pltpu.VMEM)
ANY = pl.BlockSpec(memory_space=pl.ANY)
NZ, NY, NX = 8, 2, 4
TILE, F, SLOTS, TROWS, TCOLS = 128, 256, 12, 32, 32
HALF = TROWS // 2
WHOLE = 60 << 20
LARGE = 40 << 20
SMALL = 8 << 20


def shift(value, axis, size, step):
    return lax.ppermute(value, axis, [(i, (i + step) % size) for i in range(size)])


def swap(value, axis):
    return lax.ppermute(value, axis, [(0, 1), (1, 0)])


def plane_send(value, dy, dx):
    pairs = []
    for y in range(NY):
        for x in range(NX):
            pairs.append((y * NX + x, (y + dy) % NY * NX + (x + dx) % NX))
    return lax.ppermute(value, ("yl", "x"), pairs)


PLANE = [(dy, dx) for dy in range(NY) for dx in range(NX)]


def tile_row(u, core):
    return 4 * (u >> 1) + 2 * core + (u & 1)


def start_tiles(core, adj_ref, slab, sem):
    def row_copy(u):
        return pltpu.make_async_copy(adj_ref.at[tile_row(u, core)], slab.at[u], sem.at[u])

    def start(u, carry):
        row_copy(u).start()
        return carry

    lax.fori_loop(0, HALF, start, 0)
    return lambda u: row_copy(u).wait()


def gather_pieces(meta_ref, start, pieces, held):
    for k, piece in enumerate(pieces):
        held[pl.ds(meta_ref[start + k], piece.shape[0])] = piece[...]


COLS_AT, COUNTS_AT, PLACES_AT = 0, TROWS * SLOTS, TROWS * SLOTS + TROWS
GRADS_AT = PLACES_AT + 16
SENDS_AT = GRADS_AT + 8
CORE_AT = SENDS_AT + 16


def forward_body(meta_ref, adj_ref, *rest, n, first):
    pieces = rest[:n]
    core = meta_ref[CORE_AT]
    if first:
        out_ref, panel, slab, sem, piece_sem = rest[n:]
        core = 1 - core
        copies = []
        for piece in pieces:
            for i in range(piece.shape[0] // 2):
                k = len(copies)
                copies.append(
                    pltpu.make_async_copy(
                        piece.at[pl.ds(2 * i, 2)],
                        panel.at[pl.ds(meta_ref[PLACES_AT + k], 2)],
                        piece_sem.at[k],
                    )
                )
        for copy in copies:
            copy.start()
    else:
        out_ref, slab, sem = rest[n:]
        panel = pieces[0]
    arrived = start_tiles(core, adj_ref, slab, sem)
    if first:
        for copy in copies:
            copy.wait()

    def step(u, carry):
        arrived(u)
        t = tile_row(u, core)
        count = meta_ref[COUNTS_AT + t]
        pairs = (count + 1) >> 1
        for p in range(1, SLOTS // 2 + 1):

            @pl.when(pairs == p)
            def _(p=p):
                left = [slab[u, s] for s in range(2 * p)]
                left[-1] = jnp.where(count == 2 * p, left[-1], jnp.zeros_like(left[-1]))
                right = [panel[meta_ref[COLS_AT + t * SLOTS + s]] for s in range(2 * p)]
                out_ref[u] = jnp.dot(
                    jnp.concatenate(left, 1),
                    jnp.concatenate(right, 0),
                    preferred_element_type=F32,
                ).astype(out_ref.dtype)

        return carry

    lax.fori_loop(0, HALF, step, 0)


def forward(meta, adj, pieces):
    n = len(pieces)
    first = n > 1
    panel = [jax.ShapeDtypeStruct((TCOLS, TILE, F), BF)] if first else []
    return pl.pallas_call(
        functools.partial(forward_body, n=n, first=first),
        out_shape=[jax.ShapeDtypeStruct((HALF, TILE, F), BF if first else F32)] + panel,
        in_specs=[SM, ANY] + ([ANY] * n if first else [VM]),
        out_specs=[VM] * (1 + len(panel)),
        scratch_shapes=[
            pltpu.VMEM((HALF, SLOTS, TILE, TILE), BF),
            pltpu.SemaphoreType.DMA((HALF,)),
        ]
        + ([pltpu.SemaphoreType.DMA((TCOLS // 2,))] if first else []),
        compiler_params=pltpu.CompilerParams(vmem_limit_bytes=WHOLE if first else LARGE),
        cost_estimate=pl.CostEstimate(flops=4 * 10**9, bytes_accessed=9 << 20, transcendentals=0),
        name="forward",
    )(meta, adj, *pieces)


def backward_body(meta_ref, adj_ref, *rest, n, first):
    pieces = rest[:n]
    core = meta_ref[CORE_AT]
    if first:
        acc, held, slab, sem = rest[n:]
    else:
        core = 1 - core
        prior_ref = rest[n]
        m = len(SENDS)
        outs = rest[n + 1 : n + 1 + m]
        held, slab, sem, acc = rest[n + 1 + m :]
    arrived = start_tiles(core, adj_ref, slab, sem)
    gather_pieces(meta_ref, GRADS_AT, pieces, held)
    acc[...] = jnp.zeros_like(acc)

    def step(u, carry):
        arrived(u)
        t = tile_row(u, core)
        count = meta_ref[COUNTS_AT + t]
        pairs = (count + 1) >> 1
        for p in range(1, SLOTS // 2 + 1):

            @pl.when(pairs == p)
            def _(p=p):
                grad = held[u]
                for q in range(p):
                    a0, a1 = slab[u, 2 * q], slab[u, 2 * q + 1]
                    if q == p - 1:
                        a1 = jnp.where(count == 2 * p, a1, jnp.zeros_like(a1))
                    terms = jnp.dot(grad, jnp.concatenate([a0, a1], 1), preferred_element_type=F32)
                    acc[meta_ref[COLS_AT + t * SLOTS + 2 * q]] += terms[:, :TILE]
                    acc[meta_ref[COLS_AT + t * SLOTS + 2 * q + 1]] += terms[:, TILE:]

        return carry

    lax.fori_loop(0, HALF, step, 0)
    if not first:
        k = SENDS_AT
        for out, (steps, _) in zip(outs, SENDS):
            for j in range(len(steps)):
                for i in range(2):
                    place = meta_ref[k] + i
                    out[j, i] = (acc[place] + prior_ref[place]).astype(out.dtype)
                k += 1


SENDS = [((k, -k) if k in (1, 2, 3) else (k,), across) for across in (1, 0) for k in (4, 3, 2, 1, 0)]


def backward(meta, adj, pieces, prior=None):
    n = len(pieces)
    first = prior is None
    scratch = [
        pltpu.VMEM((HALF, F, TILE), BF),
        pltpu.VMEM((HALF, SLOTS, TILE, TILE), BF),
        pltpu.SemaphoreType.DMA((HALF,)),
    ]
    if first:
        out_shape = jax.ShapeDtypeStruct((TCOLS, F, TILE), F32)
        out_specs = VM
        extra = []
    else:
        out_shape = [
            jax.ShapeDtypeStruct((len(steps), 2, F, TILE), BF if across else F32)
            for steps, across in SENDS
        ]
        out_specs = [VM] * len(SENDS)
        scratch.append(pltpu.VMEM((TCOLS, F, TILE), F32))
        extra = [prior]
    return pl.pallas_call(
        functools.partial(backward_body, n=n, first=first),
        out_shape=out_shape,
        in_specs=[SM, ANY] + [VM] * n + [VM] * len(extra),
        out_specs=out_specs,
        scratch_shapes=scratch,
        compiler_params=pltpu.CompilerParams(vmem_limit_bytes=LARGE),
        cost_estimate=pl.CostEstimate(flops=4 * 10**9, bytes_accessed=9 << 20, transcendentals=0),
        name="backward",
    )(meta, adj, *pieces, *extra)


def pair_add_body(at_ref, mine_ref, other_ref, *outs):
    for k, out in enumerate(outs):
        rows = pl.ds(at_ref[k], 2)
        out[...] = (mine_ref[rows].astype(F32) + other_ref[rows].astype(F32)).astype(out.dtype)


def pair_add(at, mine, other):
    return pl.pallas_call(
        pair_add_body,
        out_shape=[jax.ShapeDtypeStruct((2, TILE, F), BF if any(to) else F32) for to in PLANE],
        in_specs=[SM, VM, VM],
        out_specs=[VM] * len(PLANE),
        compiler_params=pltpu.CompilerParams(vmem_limit_bytes=SMALL),
        name="pair_add",
    )(at, mine, other)


def middle_body(*refs):
    n = len(PLANE)
    pieces = refs[:n]
    weight_ref, cotangent_ref, act_ref, grad_ref = refs[n:]
    total = pieces[0][...].astype(F32)
    for piece in pieces[1:]:
        total = total + piece[...].astype(F32)
    aggregated = total.astype(BF).reshape(2 * TILE, F)
    weight = weight_ref[...]
    pre = jnp.dot(aggregated, weight, preferred_element_type=F32)
    sigma = jax.nn.sigmoid(pre)
    act_ref[...] = (pre * sigma).astype(BF)
    slope = sigma * (1.0 + pre * (1.0 - sigma))
    pre_grad = (cotangent_ref[...].astype(F32) * slope).astype(BF)
    grad = lax.dot_general(
        weight, pre_grad, (((1,), (1,)), ((), ())), preferred_element_type=F32
    ).astype(BF)
    grad_ref[0] = grad[:, :TILE]
    grad_ref[1] = grad[:, TILE:]


def middle(pieces, weight, cotangent):
    return pl.pallas_call(
        middle_body,
        out_shape=[
            jax.ShapeDtypeStruct((2 * TILE, F), BF),
            jax.ShapeDtypeStruct((2, F, TILE), BF),
        ],
        in_specs=[VM] * (len(pieces) + 2),
        out_specs=[VM, VM],
        compiler_params=pltpu.CompilerParams(vmem_limit_bytes=SMALL),
        name="middle",
    )(*pieces, weight, cotangent)


def finish_body(own_ref, far_ref, *rest):
    out_ref = rest[-1]
    for i in range(2):
        total = own_ref[0, i] + far_ref[0, i].astype(F32)
        for ref in rest[:-1]:
            total = total + ref[i].astype(F32)
        out_ref[pl.ds(i * TILE, TILE), :] = total.T.astype(BF)


def finish(*terms):
    return pl.pallas_call(
        finish_body,
        out_shape=jax.ShapeDtypeStruct((2 * TILE, F), BF),
        in_specs=[VM] * len(terms),
        out_specs=VM,
        compiler_params=pltpu.CompilerParams(vmem_limit_bytes=SMALL),
        name="finish",
    )(*terms)


def add(*terms):
    total = terms[0].astype(F32)
    for term in terms[1:]:
        total = total + term.astype(F32)
    return total.astype(BF)


def local(features, adj_tiles, tile_cols, tile_count, weight, cotangent):
    yh, z = lax.axis_index("yh"), lax.axis_index("z")
    yl, x, core = lax.axis_index("yl"), lax.axis_index("x"), lax.axis_index("c")

    adj = adj_tiles[0]
    own = features.reshape(2, TILE, F)
    pieces, places = [], []

    def keep(piece, half, *steps):
        pieces.append(piece)
        for step in steps:
            places.append(2 * (half * NZ + (z - step) % NZ))

    keep(own, yh, 0)
    keep(swap(own, "yh"), 1 - yh, 0)
    up = down = own
    for step in range(1, NZ // 2):
        up, down = shift(up, "z", NZ, 1), shift(down, "z", NZ, -1)
        both = jnp.concatenate([up, down], 0)
        keep(both, yh, step, -step)
        keep(swap(both, "yh"), 1 - yh, step, -step)
    up = shift(up, "z", NZ, 1)
    keep(up, yh, NZ // 2)
    keep(swap(up, "yh"), 1 - yh, NZ // 2)
    grad_at = [2 * ((yl - dy) % NY * NX + (x - dx) % NX) for dy, dx in PLANE]
    send = [
        2 * ((yh + across) % 2 * NZ + (z + step) % NZ) for steps, across in SENDS for step in steps
    ]
    meta = jnp.concatenate(
        [
            tile_cols[0].reshape(-1),
            tile_count[0].reshape(-1),
            jnp.stack(places + grad_at + send + [core]).astype(jnp.int32),
        ]
    )
    dests = jnp.stack([2 * ((yl + dy) % NY * NX + (x + dx) % NX) for dy, dx in PLANE]).astype(jnp.int32)

    for_other, panel = forward(meta, adj, pieces)
    theirs = swap(for_other, "c")
    (for_mine,) = forward(meta, adj, [panel])
    parts = pair_add(dests, for_mine, theirs)
    parts = [parts[0]] + [plane_send(part, dy, dx) for part, (dy, dx) in list(zip(parts, PLANE))[1:]]
    activation, grad = middle(parts, weight, cotangent)

    grads = [grad] + [plane_send(grad, dy, dx) for dy, dx in PLANE[1:]]
    grads_other = [swap(piece, "c") for piece in grads]
    half_sum = backward(meta, adj, grads)
    far4, far3, far2, far1, far0, own4, own3, own2, own1, own0 = backward(
        meta, adj, grads_other, half_sum
    )

    far4, far3 = swap(far4, "yh"), swap(far3, "yh")
    up = shift(add(own4[0], far4[0]), "z", NZ, 1)
    far2, _ = lax.optimization_barrier((far2, far4))
    far2 = swap(far2, "yh")
    down = shift(add(own3[1], far3[1]), "z", NZ, -1)
    up = shift(add(own3[0], far3[0], up), "z", NZ, 1)
    far1, _ = lax.optimization_barrier((far1, far3))
    far1 = swap(far1, "yh")
    up = shift(add(own2[0], far2[0], up), "z", NZ, 1)
    down = shift(add(own2[1], far2[1], down), "z", NZ, -1)
    far0, _ = lax.optimization_barrier((far0, far2))
    far0 = swap(far0, "yh")
    up = shift(add(own1[0], far1[0], up), "z", NZ, 1)
    down = shift(add(own1[1], far1[1], down), "z", NZ, -1)
    feature_grad = finish(own0, far0, up, down)
    return activation, feature_grad


def solution(mesh):
    fine = Mesh(mesh.devices.reshape(2, NZ, NY, NX, 2), ("yh", "z", "yl", "x", "c"))
    row, col = ("yh", "z"), ("yl", "x", "c")
    in_specs = (
        P(col + row, None),
        P(col, row, None, None, None),
        P(col, row, None),
        P(col, row),
        P(),
        P(row + col, None),
    )
    out_specs = (P(row + col, None), P(col + row, None))
    return jax.shard_map(local, mesh=fine, in_specs=in_specs, out_specs=out_specs, check_vma=False)
```

```python
import functools

import jax
import jax.numpy as jnp
from jax import lax
from jax.experimental import pallas as pl
from jax.experimental.pallas import tpu as pltpu
from jax.sharding import Mesh
from jax.sharding import PartitionSpec as P

BF = jnp.bfloat16
F32 = jnp.float32
SM = pl.BlockSpec(memory_space=pltpu.SMEM)
VM = pl.BlockSpec(memory_space=pltpu.VMEM)
ANY = pl.BlockSpec(memory_space=pl.ANY)
NZ, NY, NX = 8, 2, 4
TILE, F, SLOTS, TROWS, TCOLS = 128, 256, 12, 32, 32
HALF = TROWS // 2
WHOLE = 60 << 20
LARGE = 40 << 20
SMALL = 8 << 20


def shift(value, axis, size, step):
    return lax.ppermute(value, axis, [(i, (i + step) % size) for i in range(size)])


def swap(value, axis):
    return lax.ppermute(value, axis, [(0, 1), (1, 0)])


def plane_send(value, dy, dx):
    pairs = []
    for y in range(NY):
        for x in range(NX):
            pairs.append((y * NX + x, (y + dy) % NY * NX + (x + dx) % NX))
    return lax.ppermute(value, ("yl", "x"), pairs)


PLANE = [(dy, dx) for dy in range(NY) for dx in range(NX)]


def tile_row(u, core):
    return 4 * (u >> 1) + 2 * core + (u & 1)


def start_tiles(rows, tile_row_of, meta_ref, adj_ref, slab, sem):
    def each(u, act):
        t = tile_row_of(u)
        quads = (meta_ref[COUNTS_AT + t] + 3) >> 2
        for q in range(1, SLOTS // 4 + 1):

            @pl.when(quads == q)
            def _(q=q):
                live = pl.ds(0, 4 * q)
                act(pltpu.make_async_copy(adj_ref.at[t, live], slab.at[u, live], sem.at[u]))

    def start(u, carry):
        each(u, lambda copy: copy.start())
        return carry

    lax.fori_loop(0, rows, start, 0)
    return lambda u: each(u, lambda copy: copy.wait())


def gather_pieces(meta_ref, start, pieces, held):
    for k, piece in enumerate(pieces):
        held[pl.ds(meta_ref[start + k], piece.shape[0])] = piece[...]


COLS_AT, COUNTS_AT, PLACES_AT = 0, TROWS * SLOTS, TROWS * SLOTS + TROWS
GRADS_AT = PLACES_AT + 16
SENDS_AT = GRADS_AT + 16
CORE_AT = SENDS_AT + 16


def forward_body(meta_ref, adj_ref, *rest, n, first):
    pieces = rest[:n]
    core = meta_ref[CORE_AT]
    if first:
        out_ref, panel, slab, sem, piece_sem = rest[n:]
        core = 1 - core
        copies = []
        for piece in pieces:
            for i in range(piece.shape[0] // 2):
                k = len(copies)
                copies.append(
                    pltpu.make_async_copy(
                        piece.at[pl.ds(2 * i, 2)],
                        panel.at[pl.ds(meta_ref[PLACES_AT + k], 2)],
                        piece_sem.at[k],
                    )
                )
        for copy in copies:
            copy.start()
    else:
        out_ref, slab, sem = rest[n:]
        panel = pieces[0]
    arrived = start_tiles(HALF, lambda u: tile_row(u, core), meta_ref, adj_ref, slab, sem)
    if first:
        for copy in copies:
            copy.wait()

    def step(u, carry):
        arrived(u)
        t = tile_row(u, core)
        count = meta_ref[COUNTS_AT + t]
        pairs = (count + 1) >> 1
        for p in range(1, SLOTS // 2 + 1):

            @pl.when(pairs == p)
            def _(p=p):
                left = [slab[u, s] for s in range(2 * p)]
                left[-1] = jnp.where(count == 2 * p, left[-1], jnp.zeros_like(left[-1]))
                right = [panel[meta_ref[COLS_AT + t * SLOTS + s]] for s in range(2 * p)]
                out_ref[u] = jnp.dot(
                    jnp.concatenate(left, 1),
                    jnp.concatenate(right, 0),
                    preferred_element_type=F32,
                ).astype(out_ref.dtype)

        return carry

    lax.fori_loop(0, HALF, step, 0)


def forward(meta, adj, pieces):
    n = len(pieces)
    first = n > 1
    panel = [jax.ShapeDtypeStruct((TCOLS, TILE, F), BF)] if first else []
    return pl.pallas_call(
        functools.partial(forward_body, n=n, first=first),
        out_shape=[jax.ShapeDtypeStruct((HALF, TILE, F), BF if first else F32)] + panel,
        in_specs=[SM, ANY] + ([ANY] * n if first else [VM]),
        out_specs=[VM] * (1 + len(panel)),
        scratch_shapes=[
            pltpu.VMEM((HALF, SLOTS, TILE, TILE), BF),
            pltpu.SemaphoreType.DMA((HALF,)),
        ]
        + ([pltpu.SemaphoreType.DMA((TCOLS // 2,))] if first else []),
        compiler_params=pltpu.CompilerParams(vmem_limit_bytes=WHOLE if first else LARGE),
        cost_estimate=pl.CostEstimate(flops=4 * 10**9, bytes_accessed=9 << 20, transcendentals=0),
        name="forward",
    )(meta, adj, *pieces)


def backward_body(meta_ref, adj_ref, *rest, n):
    pieces = rest[:n]
    outs = rest[n : n + len(SENDS)]
    held, slab, sem, acc = rest[n + len(SENDS) :]
    arrived = start_tiles(TROWS, lambda t: t, meta_ref, adj_ref, slab, sem)
    gather_pieces(meta_ref, GRADS_AT, pieces, held)
    acc[...] = jnp.zeros_like(acc)

    def step(t, carry):
        arrived(t)
        count = meta_ref[COUNTS_AT + t]
        pairs = (count + 1) >> 1
        for p in range(1, SLOTS // 2 + 1):

            @pl.when(pairs == p)
            def _(p=p):
                grad = held[t]
                for q in range(p):
                    a0, a1 = slab[t, 2 * q], slab[t, 2 * q + 1]
                    if q == p - 1:
                        a1 = jnp.where(count == 2 * p, a1, jnp.zeros_like(a1))
                    terms = jnp.dot(grad, jnp.concatenate([a0, a1], 1), preferred_element_type=F32)
                    acc[meta_ref[COLS_AT + t * SLOTS + 2 * q]] += terms[:, :TILE]
                    acc[meta_ref[COLS_AT + t * SLOTS + 2 * q + 1]] += terms[:, TILE:]

        return carry

    lax.fori_loop(0, TROWS, step, 0)
    k = SENDS_AT
    for out, (steps, _) in zip(outs, SENDS):
        for j in range(len(steps)):
            for i in range(2):
                out[j, i] = acc[meta_ref[k] + i].astype(out.dtype)
            k += 1


SENDS = [((k, -k) if k in (1, 2, 3) else (k,), across) for across in (1, 0) for k in (4, 3, 2, 1, 0)]


def backward(meta, adj, pieces):
    n = len(pieces)
    return pl.pallas_call(
        functools.partial(backward_body, n=n),
        out_shape=[
            jax.ShapeDtypeStruct((len(steps), 2, F, TILE), BF if across else F32)
            for steps, across in SENDS
        ],
        in_specs=[SM, ANY] + [VM] * n,
        out_specs=[VM] * len(SENDS),
        scratch_shapes=[
            pltpu.VMEM((TROWS, F, TILE), BF),
            pltpu.VMEM((TROWS, SLOTS, TILE, TILE), BF),
            pltpu.SemaphoreType.DMA((TROWS,)),
            pltpu.VMEM((TCOLS, F, TILE), F32),
        ],
        compiler_params=pltpu.CompilerParams(vmem_limit_bytes=LARGE),
        cost_estimate=pl.CostEstimate(flops=8 * 10**9, bytes_accessed=18 << 20, transcendentals=0),
        name="backward",
    )(meta, adj, *pieces)


def pair_add_body(at_ref, mine_ref, other_ref, *outs):
    for k, out in enumerate(outs):
        rows = pl.ds(at_ref[k], 2)
        out[...] = (mine_ref[rows].astype(F32) + other_ref[rows].astype(F32)).astype(out.dtype)


def pair_add(at, mine, other):
    return pl.pallas_call(
        pair_add_body,
        out_shape=[jax.ShapeDtypeStruct((2, TILE, F), BF if any(to) else F32) for to in PLANE],
        in_specs=[SM, VM, VM],
        out_specs=[VM] * len(PLANE),
        compiler_params=pltpu.CompilerParams(vmem_limit_bytes=SMALL),
        name="pair_add",
    )(at, mine, other)


def middle_body(*refs):
    n = len(PLANE)
    pieces = refs[:n]
    weight_ref, cotangent_ref, act_ref, grad_ref = refs[n:]
    total = pieces[0][...].astype(F32)
    for piece in pieces[1:]:
        total = total + piece[...].astype(F32)
    aggregated = total.astype(BF).reshape(2 * TILE, F)
    weight = weight_ref[...]
    pre = jnp.dot(aggregated, weight, preferred_element_type=F32)
    sigma = jax.nn.sigmoid(pre)
    act_ref[...] = (pre * sigma).astype(BF)
    slope = sigma * (1.0 + pre * (1.0 - sigma))
    pre_grad = (cotangent_ref[...].astype(F32) * slope).astype(BF)
    grad = lax.dot_general(
        weight, pre_grad, (((1,), (1,)), ((), ())), preferred_element_type=F32
    ).astype(BF)
    grad_ref[0] = grad[:, :TILE]
    grad_ref[1] = grad[:, TILE:]


def middle(pieces, weight, cotangent):
    return pl.pallas_call(
        middle_body,
        out_shape=[
            jax.ShapeDtypeStruct((2 * TILE, F), BF),
            jax.ShapeDtypeStruct((2, F, TILE), BF),
        ],
        in_specs=[VM] * (len(pieces) + 2),
        out_specs=[VM, VM],
        compiler_params=pltpu.CompilerParams(vmem_limit_bytes=SMALL),
        name="middle",
    )(*pieces, weight, cotangent)


def finish_body(own_ref, far_ref, *rest):
    out_ref = rest[-1]
    for i in range(2):
        total = own_ref[0, i] + far_ref[0, i].astype(F32)
        for ref in rest[:-1]:
            total = total + ref[i].astype(F32)
        out_ref[pl.ds(i * TILE, TILE), :] = total.T.astype(BF)


def finish(*terms):
    return pl.pallas_call(
        finish_body,
        out_shape=jax.ShapeDtypeStruct((2 * TILE, F), BF),
        in_specs=[VM] * len(terms),
        out_specs=VM,
        compiler_params=pltpu.CompilerParams(vmem_limit_bytes=SMALL),
        name="finish",
    )(*terms)


def add(*terms):
    total = terms[0].astype(F32)
    for term in terms[1:]:
        total = total + term.astype(F32)
    return total.astype(BF)


def local(features, adj_tiles, tile_cols, tile_count, weight, cotangent):
    yh, z = lax.axis_index("yh"), lax.axis_index("z")
    yl, x, core = lax.axis_index("yl"), lax.axis_index("x"), lax.axis_index("c")

    adj = adj_tiles[0]
    own = features.reshape(2, TILE, F)
    pieces, places = [], []

    def keep(piece, half, *steps):
        pieces.append(piece)
        for step in steps:
            places.append(2 * (half * NZ + (z - step) % NZ))

    keep(own, yh, 0)
    keep(swap(own, "yh"), 1 - yh, 0)
    up = down = own
    for step in range(1, NZ // 2):
        up, down = shift(up, "z", NZ, 1), shift(down, "z", NZ, -1)
        both = jnp.concatenate([up, down], 0)
        keep(both, yh, step, -step)
        keep(swap(both, "yh"), 1 - yh, step, -step)
    up = shift(up, "z", NZ, 1)
    keep(up, yh, NZ // 2)
    keep(swap(up, "yh"), 1 - yh, NZ // 2)
    grad_at = [
        2 * (2 * ((yl - dy) % NY * NX + (x - dx) % NX) + side)
        for side in (core, 1 - core)
        for dy, dx in PLANE
    ]
    send = [
        2 * ((yh + across) % 2 * NZ + (z + step) % NZ) for steps, across in SENDS for step in steps
    ]
    meta = jnp.concatenate(
        [
            tile_cols[0].reshape(-1),
            tile_count[0].reshape(-1),
            jnp.stack(places + grad_at + send + [core]).astype(jnp.int32),
        ]
    )
    dests = jnp.stack([2 * ((yl + dy) % NY * NX + (x + dx) % NX) for dy, dx in PLANE]).astype(jnp.int32)

    for_other, panel = forward(meta, adj, pieces)
    theirs = swap(for_other, "c")
    (for_mine,) = forward(meta, adj, [panel])
    parts = pair_add(dests, for_mine, theirs)
    parts = [parts[0]] + [plane_send(part, dy, dx) for part, (dy, dx) in list(zip(parts, PLANE))[1:]]
    activation, grad = middle(parts, weight, cotangent)

    grads = [grad] + [plane_send(grad, dy, dx) for dy, dx in PLANE[1:]]
    grads_other = [swap(piece, "c") for piece in grads]
    far4, far3, far2, far1, far0, own4, own3, own2, own1, own0 = backward(
        meta, adj, grads + grads_other
    )

    far4, far3 = swap(far4, "yh"), swap(far3, "yh")
    up = shift(add(own4[0], far4[0]), "z", NZ, 1)
    far2, _ = lax.optimization_barrier((far2, far4))
    far2 = swap(far2, "yh")
    down = shift(add(own3[1], far3[1]), "z", NZ, -1)
    up = shift(add(own3[0], far3[0], up), "z", NZ, 1)
    far1, _ = lax.optimization_barrier((far1, far3))
    far1 = swap(far1, "yh")
    up = shift(add(own2[0], far2[0], up), "z", NZ, 1)
    down = shift(add(own2[1], far2[1], down), "z", NZ, -1)
    far0, _ = lax.optimization_barrier((far0, far2))
    far0 = swap(far0, "yh")
    up = shift(add(own1[0], far1[0], up), "z", NZ, 1)
    down = shift(add(own1[1], far1[1], down), "z", NZ, -1)
    feature_grad = finish(own0, far0, up, down)
    return activation, feature_grad


def solution(mesh):
    fine = Mesh(mesh.devices.reshape(2, NZ, NY, NX, 2), ("yh", "z", "yl", "x", "c"))
    row, col = ("yh", "z"), ("yl", "x", "c")
    in_specs = (
        P(col + row, None),
        P(col, row, None, None, None),
        P(col, row, None),
        P(col, row),
        P(),
        P(row + col, None),
    )
    out_specs = (P(row + col, None), P(col + row, None))
    return jax.shard_map(local, mesh=fine, in_specs=in_specs, out_specs=out_specs, check_vma=False)
```

```python
import functools

import jax
import jax.numpy as jnp
from jax import lax
from jax.experimental import pallas as pl
from jax.experimental.pallas import tpu as pltpu
from jax.sharding import Mesh
from jax.sharding import PartitionSpec as P

BF = jnp.bfloat16
F32 = jnp.float32
SM = pl.BlockSpec(memory_space=pltpu.SMEM)
VM = pl.BlockSpec(memory_space=pltpu.VMEM)
ANY = pl.BlockSpec(memory_space=pl.ANY)
NZ, NY, NX = 8, 2, 4
TILE, F, SLOTS, TROWS, TCOLS = 128, 256, 12, 32, 32
HALF = TROWS // 2
WHOLE = 60 << 20
LARGE = 40 << 20
SMALL = 8 << 20


def shift(value, axis, size, step):
    return lax.ppermute(value, axis, [(i, (i + step) % size) for i in range(size)])


def swap(value, axis):
    return lax.ppermute(value, axis, [(0, 1), (1, 0)])


def plane_send(value, dy, dx):
    pairs = []
    for y in range(NY):
        for x in range(NX):
            pairs.append((y * NX + x, (y + dy) % NY * NX + (x + dx) % NX))
    return lax.ppermute(value, ("yl", "x"), pairs)


PLANE = [(0, 0), (0, 1), (1, 1), (0, 3), (1, 3), (0, 2), (1, 0), (1, 2)]


def tile_row(u, core):
    return 4 * (u >> 1) + 2 * core + (u & 1)


def start_tiles(rows, tile_row_of, meta_ref, adj_ref, slab, sem):
    def each(u, act):
        t = tile_row_of(u)
        quads = (meta_ref[COUNTS_AT + t] + 3) >> 2
        for q in range(1, SLOTS // 4 + 1):

            @pl.when(quads == q)
            def _(q=q):
                live = pl.ds(0, 4 * q)
                act(pltpu.make_async_copy(adj_ref.at[t, live], slab.at[u, live], sem.at[u]))

    def start(u, carry):
        each(u, lambda copy: copy.start())
        return carry

    lax.fori_loop(0, rows, start, 0)
    return lambda u: each(u, lambda copy: copy.wait())


def gather_pieces(meta_ref, start, pieces, held):
    for k, piece in enumerate(pieces):
        held[pl.ds(meta_ref[start + k], piece.shape[0])] = piece[...]


COLS_AT, COUNTS_AT, PLACES_AT = 0, TROWS * SLOTS, TROWS * SLOTS + TROWS
GRADS_AT = PLACES_AT + 16
SENDS_AT = GRADS_AT + 16
CORE_AT = SENDS_AT + 16


def forward_body(meta_ref, adj_ref, *rest, n, first):
    pieces = rest[:n]
    core = meta_ref[CORE_AT]
    if first:
        out_ref, panel, slab, sem, piece_sem = rest[n:]
        core = 1 - core
        copies = []
        for piece in pieces:
            for i in range(piece.shape[0] // 2):
                k = len(copies)
                copies.append(
                    pltpu.make_async_copy(
                        piece.at[pl.ds(2 * i, 2)],
                        panel.at[pl.ds(meta_ref[PLACES_AT + k], 2)],
                        piece_sem.at[k],
                    )
                )
        for copy in copies:
            copy.start()
    else:
        out_ref, slab, sem = rest[n:]
        panel = pieces[0]
    arrived = start_tiles(HALF, lambda u: tile_row(u, core), meta_ref, adj_ref, slab, sem)
    if first:
        for copy in copies:
            copy.wait()

    def step(u, carry):
        arrived(u)
        t = tile_row(u, core)
        count = meta_ref[COUNTS_AT + t]
        pairs = (count + 1) >> 1
        for p in range(1, SLOTS // 2 + 1):

            @pl.when(pairs == p)
            def _(p=p):
                left = [slab[u, s] for s in range(2 * p)]
                left[-1] = jnp.where(count == 2 * p, left[-1], jnp.zeros_like(left[-1]))
                right = [panel[meta_ref[COLS_AT + t * SLOTS + s]] for s in range(2 * p)]
                out_ref[u] = jnp.dot(
                    jnp.concatenate(left, 1),
                    jnp.concatenate(right, 0),
                    preferred_element_type=F32,
                ).astype(out_ref.dtype)

        return carry

    lax.fori_loop(0, HALF, step, 0)


def forward(meta, adj, pieces):
    n = len(pieces)
    first = n > 1
    panel = [jax.ShapeDtypeStruct((TCOLS, TILE, F), BF)] if first else []
    return pl.pallas_call(
        functools.partial(forward_body, n=n, first=first),
        out_shape=[jax.ShapeDtypeStruct((HALF, TILE, F), BF if first else F32)] + panel,
        in_specs=[SM, ANY] + ([ANY] * n if first else [VM]),
        out_specs=[VM] * (1 + len(panel)),
        scratch_shapes=[
            pltpu.VMEM((HALF, SLOTS, TILE, TILE), BF),
            pltpu.SemaphoreType.DMA((HALF,)),
        ]
        + ([pltpu.SemaphoreType.DMA((TCOLS // 2,))] if first else []),
        compiler_params=pltpu.CompilerParams(vmem_limit_bytes=WHOLE if first else LARGE),
        cost_estimate=pl.CostEstimate(flops=4 * 10**9, bytes_accessed=9 << 20, transcendentals=0),
        name="forward",
    )(meta, adj, *pieces)


def backward_body(meta_ref, adj_ref, *rest, n):
    pieces = rest[:n]
    outs = rest[n : n + len(SENDS)]
    held, slab, sem, acc = rest[n + len(SENDS) :]
    arrived = start_tiles(TROWS, lambda t: t, meta_ref, adj_ref, slab, sem)
    gather_pieces(meta_ref, GRADS_AT, pieces, held)
    acc[...] = jnp.zeros_like(acc)

    def step(t, carry):
        arrived(t)
        count = meta_ref[COUNTS_AT + t]
        pairs = (count + 1) >> 1
        for p in range(1, SLOTS // 2 + 1):

            @pl.when(pairs == p)
            def _(p=p):
                grad = held[t]
                for q in range(p):
                    a0, a1 = slab[t, 2 * q], slab[t, 2 * q + 1]
                    if q == p - 1:
                        a1 = jnp.where(count == 2 * p, a1, jnp.zeros_like(a1))
                    terms = jnp.dot(grad, jnp.concatenate([a0, a1], 1), preferred_element_type=F32)
                    acc[meta_ref[COLS_AT + t * SLOTS + 2 * q]] += terms[:, :TILE]
                    acc[meta_ref[COLS_AT + t * SLOTS + 2 * q + 1]] += terms[:, TILE:]

        return carry

    lax.fori_loop(0, TROWS, step, 0)
    k = SENDS_AT
    for out, (steps, _) in zip(outs, SENDS):
        for j in range(len(steps)):
            for i in range(2):
                out[j, i] = acc[meta_ref[k] + i].astype(out.dtype)
            k += 1


SENDS = [((k, -k) if k in (1, 2, 3) else (k,), across) for across in (1, 0) for k in (4, 3, 2, 1, 0)]


def backward(meta, adj, pieces):
    n = len(pieces)
    return pl.pallas_call(
        functools.partial(backward_body, n=n),
        out_shape=[
            jax.ShapeDtypeStruct((len(steps), 2, F, TILE), BF if across else F32)
            for steps, across in SENDS
        ],
        in_specs=[SM, ANY] + [VM] * n,
        out_specs=[VM] * len(SENDS),
        scratch_shapes=[
            pltpu.VMEM((TROWS, F, TILE), BF),
            pltpu.VMEM((TROWS, SLOTS, TILE, TILE), BF),
            pltpu.SemaphoreType.DMA((TROWS,)),
            pltpu.VMEM((TCOLS, F, TILE), F32),
        ],
        compiler_params=pltpu.CompilerParams(vmem_limit_bytes=LARGE),
        cost_estimate=pl.CostEstimate(flops=8 * 10**9, bytes_accessed=18 << 20, transcendentals=0),
        name="backward",
    )(meta, adj, *pieces)


def pair_add_body(at_ref, mine_ref, other_ref, *outs):
    for k, out in enumerate(outs):
        rows = pl.ds(at_ref[k], 2)
        out[...] = (mine_ref[rows].astype(F32) + other_ref[rows].astype(F32)).astype(out.dtype)


def pair_add(at, mine, other):
    return pl.pallas_call(
        pair_add_body,
        out_shape=[jax.ShapeDtypeStruct((2, TILE, F), BF if any(to) else F32) for to in PLANE],
        in_specs=[SM, VM, VM],
        out_specs=[VM] * len(PLANE),
        compiler_params=pltpu.CompilerParams(vmem_limit_bytes=SMALL),
        name="pair_add",
    )(at, mine, other)


def middle_body(*refs):
    n = len(PLANE)
    pieces = refs[:n]
    weight_ref, cotangent_ref, act_ref, grad_ref = refs[n:]
    total = pieces[0][...].astype(F32)
    for piece in pieces[1:]:
        total = total + piece[...].astype(F32)
    aggregated = total.astype(BF).reshape(2 * TILE, F)
    weight = weight_ref[...]
    pre = jnp.dot(aggregated, weight, preferred_element_type=F32)
    sigma = jax.nn.sigmoid(pre)
    act_ref[...] = (pre * sigma).astype(BF)
    slope = sigma * (1.0 + pre * (1.0 - sigma))
    pre_grad = (cotangent_ref[...].astype(F32) * slope).astype(BF)
    grad = lax.dot_general(
        weight, pre_grad, (((1,), (1,)), ((), ())), preferred_element_type=F32
    ).astype(BF)
    grad_ref[0] = grad[:, :TILE]
    grad_ref[1] = grad[:, TILE:]


def middle(pieces, weight, cotangent):
    return pl.pallas_call(
        middle_body,
        out_shape=[
            jax.ShapeDtypeStruct((2 * TILE, F), BF),
            jax.ShapeDtypeStruct((2, F, TILE), BF),
        ],
        in_specs=[VM] * (len(pieces) + 2),
        out_specs=[VM, VM],
        compiler_params=pltpu.CompilerParams(vmem_limit_bytes=SMALL),
        name="middle",
    )(*pieces, weight, cotangent)


def finish_body(own_ref, far_ref, *rest):
    out_ref = rest[-1]
    for i in range(2):
        total = own_ref[0, i] + far_ref[0, i].astype(F32)
        for ref in rest[:-1]:
            total = total + ref[i].astype(F32)
        out_ref[pl.ds(i * TILE, TILE), :] = total.T.astype(BF)


def finish(*terms):
    return pl.pallas_call(
        finish_body,
        out_shape=jax.ShapeDtypeStruct((2 * TILE, F), BF),
        in_specs=[VM] * len(terms),
        out_specs=VM,
        compiler_params=pltpu.CompilerParams(vmem_limit_bytes=SMALL),
        name="finish",
    )(*terms)


def add(*terms):
    total = terms[0].astype(F32)
    for term in terms[1:]:
        total = total + term.astype(F32)
    return total.astype(BF)


def local(features, adj_tiles, tile_cols, tile_count, weight, cotangent):
    yh, z = lax.axis_index("yh"), lax.axis_index("z")
    yl, x, core = lax.axis_index("yl"), lax.axis_index("x"), lax.axis_index("c")

    adj = adj_tiles[0]
    own = features.reshape(2, TILE, F)
    pieces, places = [], []

    def keep(piece, half, *steps):
        pieces.append(piece)
        for step in steps:
            places.append(2 * (half * NZ + (z - step) % NZ))

    keep(own, yh, 0)
    keep(swap(own, "yh"), 1 - yh, 0)
    up = down = own
    for step in range(1, NZ // 2):
        up, down = shift(up, "z", NZ, 1), shift(down, "z", NZ, -1)
        both = jnp.concatenate([up, down], 0)
        keep(both, yh, step, -step)
        keep(swap(both, "yh"), 1 - yh, step, -step)
    up = shift(up, "z", NZ, 1)
    keep(up, yh, NZ // 2)
    keep(swap(up, "yh"), 1 - yh, NZ // 2)
    grad_at = [
        2 * (2 * ((yl - dy) % NY * NX + (x - dx) % NX) + side)
        for side in (core, 1 - core)
        for dy, dx in PLANE
    ]
    send = [
        2 * ((yh + across) % 2 * NZ + (z + step) % NZ) for steps, across in SENDS for step in steps
    ]
    meta = jnp.concatenate(
        [
            tile_cols[0].reshape(-1),
            tile_count[0].reshape(-1),
            jnp.stack(places + grad_at + send + [core]).astype(jnp.int32),
        ]
    )
    dests = jnp.stack([2 * ((yl + dy) % NY * NX + (x + dx) % NX) for dy, dx in PLANE]).astype(jnp.int32)

    for_other, panel = forward(meta, adj, pieces)
    theirs = swap(for_other, "c")
    (for_mine,) = forward(meta, adj, [panel])
    parts = pair_add(dests, for_mine, theirs)
    parts = [parts[0]] + [plane_send(part, dy, dx) for part, (dy, dx) in list(zip(parts, PLANE))[1:]]
    activation, grad = middle(parts, weight, cotangent)

    grads = [grad] + [plane_send(grad, dy, dx) for dy, dx in PLANE[1:]]
    grads_other = [swap(piece, "c") for piece in grads]
    far4, far3, far2, far1, far0, own4, own3, own2, own1, own0 = backward(
        meta, adj, grads + grads_other
    )

    far4, far3 = swap(far4, "yh"), swap(far3, "yh")
    up = shift(add(own4[0], far4[0]), "z", NZ, 1)
    far2, _ = lax.optimization_barrier((far2, far4))
    far2 = swap(far2, "yh")
    down = shift(add(own3[1], far3[1]), "z", NZ, -1)
    up = shift(add(own3[0], far3[0], up), "z", NZ, 1)
    far1, _ = lax.optimization_barrier((far1, far3))
    far1 = swap(far1, "yh")
    up = shift(add(own2[0], far2[0], up), "z", NZ, 1)
    down = shift(add(own2[1], far2[1], down), "z", NZ, -1)
    far0, _ = lax.optimization_barrier((far0, far2))
    far0 = swap(far0, "yh")
    up = shift(add(own1[0], far1[0], up), "z", NZ, 1)
    down = shift(add(own1[1], far1[1], down), "z", NZ, -1)
    feature_grad = finish(own0, far0, up, down)
    return activation, feature_grad


def solution(mesh):
    fine = Mesh(mesh.devices.reshape(2, NZ, NY, NX, 2), ("yh", "z", "yl", "x", "c"))
    row, col = ("yh", "z"), ("yl", "x", "c")
    in_specs = (
        P(col + row, None),
        P(col, row, None, None, None),
        P(col, row, None),
        P(col, row),
        P(),
        P(row + col, None),
    )
    out_specs = (P(row + col, None), P(col + row, None))
    return jax.shard_map(local, mesh=fine, in_specs=in_specs, out_specs=out_specs, check_vma=False)
```
